32 devices in a mesh: dp: 8 (over y, x, core), expert: 4 (over z).
Axes of the slice: x: 2, y: 2, z: 4, core: 2. Of those that a mesh axis runs over, the one named last changes fastest.
Arguments:
- tokens: bfloat16 [1024, 2048], P('dp'), may hold values from -6 to 6
- route_expert: int32 [1024, 4], P('dp'), may hold values from 0 to 7, all different within a row; in each aligned block of 128 rows (0 to 127, 128 to 255, ...) at most 128 rows name the same one
- route_weight: float32 [1024, 4], P('dp'), may hold values from 0.1 to 1
- gate_weight: bfloat16 [8, 1408, 2048], P('dp', 'expert'), may hold values from -0.125 to 0.125
- up_weight: bfloat16 [8, 1408, 2048], P('dp', 'expert'), may hold values from -0.125 to 0.125
- down_weight: bfloat16 [8, 1408, 2048], P('dp', 'expert'), may hold values from -0.15625 to 0.15625
- gate_scale: float32 [8, 1408], P('dp', 'expert'), may hold values from 0.5 to 2
- up_scale: float32 [8, 1408], P('dp', 'expert'), may hold values from 0.5 to 2
- down_scale: float32 [8, 2048], replicated, may hold values from 0.5 to 2
- cotangent: bfloat16 [1024, 2048], P('dp', 'expert'), may hold values from -6 to 6
Outputs:
- mixed: bfloat16 [1024, 2048], P('dp', 'expert')
- token_grad: bfloat16 [1024, 2048], P('dp', 'expert')
- route_grad: float32 [1024, 4], P('dp')
- gate_grad: float32 [8, 1408, 2048], P('dp', 'expert')
- up_grad: float32 [8, 1408, 2048], P('dp', 'expert')
- down_grad: float32 [8, 1408, 2048], P('dp', 'expert')
The draws below stay inside these ranges and needn't reach their ends.
Inputs may be any that keep to these rules, and one draw needn't show every extreme that they name: `route_expert`: each row names 4 different experts. Among the 128 rows of one aligned block (the tokens of one index of dp) no expert is named by more than 128 rows, and in some block one expert is named by exactly 128 rows.
All inputs are finite; a program needn't handle non-finite values.
Results may differ from the reference program's by a relative error of at most 0.0058.
Values may be sent and summed in bfloat16 or wider, within the bound.
A program may use at most 128 MiB of HBM per device.

```python
import math
import jax
import jax.numpy as jnp
import numpy as np
from jax import lax

D = 2048
FF = 1408
TOP = 4
TOK_DEV = 128
EXPERTS = 8
TOKENS = 1024
CAP = 128
N_DP = 8


def block_levels(own_key, shape, split, low, high):
    loudness = 1.0
    for dim, parts in split:
        heights = jax.random.uniform(jax.random.fold_in(jax.random.fold_in(own_key, 6), dim), (parts,), jnp.float32, low / len(split), high / len(split))
        loudness = loudness * jnp.repeat(jnp.exp(heights), shape[dim] // parts).reshape((-1,) + (1,) * (len(shape) - 1 - dim))
    return loudness


def deal_out(stream_key, own, number, rows, amount, top, limit, skew):
    sequence = jax.random.permutation(stream_key, amount)
    crowded, common = load_shares(amount, rows * top, limit, skew, True), load_shares(amount, rows * top, limit, skew, False)
    places = jnp.arange(amount)

    def named(tallies, offset_by):
        used = int((tallies > 0).sum())
        fixed = max(1, used // 4)
        moved = fixed + (places - fixed + offset_by * (used - fixed)) % max(1, amount - fixed)
        return jnp.zeros((amount,), jnp.int32).at[sequence[jnp.where(places < fixed, places, moved)]].set(jnp.asarray(tallies, jnp.int32))

    tallies = jnp.where(number % 4 == 0, named(crowded, number // 4), named(common, number - number // 4 - 1))
    mixed = jax.random.permutation(jax.random.fold_in(own, 3), amount)
    source_of, taker = mixed[0:amount // 2 * 2:2], mixed[1:amount // 2 * 2:2]
    margin = jnp.minimum(tallies[source_of] - 1, limit - tallies[taker]) // 2
    margin = jnp.where((source_of == sequence[0]) | (taker == sequence[0]) | (tallies[taker] == 0), 0, jnp.maximum(margin, 0))
    moved = jax.random.randint(jax.random.fold_in(own, 4), (amount // 2,), 0, 1 << 20) % (margin + 1)
    tallies = tallies.at[source_of].add(-moved).at[taker].add(moved)
    items = jnp.searchsorted(jnp.cumsum(tallies), jnp.arange(rows * top), side="right").astype(jnp.int32)
    table = items.reshape(top, rows).T
    table = table[jax.random.permutation(jax.random.fold_in(own, 1), rows)]
    offset_by = jax.random.randint(jax.random.fold_in(own, 2), (rows, 1), 0, top)
    return jnp.take_along_axis(table, (jnp.arange(top)[None, :] + offset_by) % top, axis=1)


def load_shares(number_of, total, most, lean, full):
    portions = [(1 << 20) // math.isqrt(standing ** lean) + 1 for standing in range(1, number_of + 1)]
    largest = most if full else min(most, max(-(-total // number_of), total * portions[0] // sum(portions)))
    least = 1 if total - largest >= number_of - 1 else 0
    given, spare = [largest] + [least] * (number_of - 1), total - largest - least * (number_of - 1)
    while spare > 0:
        free = [i for i in range(1, number_of) if given[i] < largest] or [i for i in range(1, number_of) if given[i] < most]
        whole, left = sum([portions[i] for i in free]), spare
        for i in free:
            extra = min(most - given[i], max(1, left * portions[i] // whole), spare)
            given[i] = given[i] + extra
            spare = spare - extra
    return np.array(given)


def bell_draw(rng, shape, deviation, limit, split=(), kind=jnp.bfloat16):
    values = jax.random.normal(rng, shape, jnp.float32) * deviation
    if len(split) > 0:
        values = block_levels(rng, shape, split, -0.22, 0.18) * values
    return jnp.clip(values, min=-limit, max=limit).astype(kind)


def setup_inputs(seed: int = 0) -> dict:
    seeds = jax.random.split(jax.random.key(seed), 11)
    tokens = bell_draw(seeds[0], (TOKENS, D), 1.0, 6.0, ((0, 8),))
    route_expert_keys = jax.random.split(jax.random.fold_in(seeds[1], 1), TOKENS // TOK_DEV)
    route_expert_turns = jax.random.permutation(jax.random.fold_in(seeds[1], 3), TOKENS // TOK_DEV)
    route_expert = jax.vmap(lambda own, number: deal_out(jax.random.fold_in(seeds[1], 2), own, number, TOK_DEV, EXPERTS, TOP, CAP, 2))(route_expert_keys, route_expert_turns).reshape((TOKENS, TOP))
    route_weight = jnp.clip(jnp.exp(math.log(1.0) - 2.3025851 * jax.random.uniform(seeds[2], (TOKENS, TOP), jnp.float32) ** block_levels(seeds[2], (TOKENS, TOP), ((0, 8),), -0.2, 0.2)), 0.1, 1.0)
    gate_weight = bell_draw(seeds[3], (EXPERTS, FF, D), D ** -0.5, 0.125, ((0, 8), (1, 4)))
    up_weight = bell_draw(seeds[4], (EXPERTS, FF, D), D ** -0.5, 0.125, ((0, 8), (1, 4)))
    down_weight = bell_draw(seeds[5], (EXPERTS, FF, D), FF ** -0.5, 0.15625, ((0, 8), (1, 4)))
    gate_scale = jnp.clip(jnp.exp(math.log(2.0) - 1.3862944 * jax.random.uniform(seeds[6], (EXPERTS, FF), jnp.float32) ** block_levels(seeds[6], (EXPERTS, FF), ((0, 8), (1, 4)), -0.2, 0.2)), 0.5, 2.0)
    up_scale = jnp.clip(jnp.exp(math.log(2.0) - 1.3862944 * jax.random.uniform(seeds[7], (EXPERTS, FF), jnp.float32) ** block_levels(seeds[7], (EXPERTS, FF), ((0, 8), (1, 4)), -0.2, 0.2)), 0.5, 2.0)
    down_scale = jnp.clip(jnp.exp(jax.random.uniform(seeds[8], (EXPERTS, D), jnp.float32, math.log(0.5), math.log(2.0))), 0.5, 2.0)
    cotangent = bell_draw(seeds[9], (TOKENS, D), 1.0, 6.0, ((0, 8), (1, 4)))
    return {"tokens": tokens, "route_expert": route_expert, "route_weight": route_weight, "gate_weight": gate_weight, "up_weight": up_weight, "down_weight": down_weight, "gate_scale": gate_scale, "up_scale": up_scale, "down_scale": down_scale, "cotangent": cotangent}


def reference(tokens, route_expert, route_weight, gate_weight, up_weight, down_weight, gate_scale, up_scale, down_scale, cotangent):
    assigned = TOKENS * TOP
    bound = N_DP * CAP
    flat_expert = route_expert.reshape(-1).astype(jnp.int32)
    flat_token = (jnp.arange(assigned, dtype=jnp.int32) // TOP).astype(jnp.int32)
    flat_weight = route_weight.reshape(-1)

    def one_expert(carry, expert_id):
        mixed_acc, input_acc, route_acc = carry
        places = jnp.nonzero(flat_expert == expert_id, size=bound, fill_value=assigned)[0].astype(jnp.int32)
        valid = places < assigned
        safe = jnp.minimum(places, assigned - 1).astype(jnp.int32)
        rows_tok = flat_token[safe]
        rows_in = jnp.where(valid[:, None], tokens[rows_tok], jnp.zeros((), tokens.dtype))
        weight_rows = jnp.where(valid, flat_weight[safe], jnp.zeros((), jnp.float32))
        gate_pre = jnp.dot(rows_in, gate_weight[expert_id].T, preferred_element_type=jnp.float32) * gate_scale[expert_id][None, :]
        up_pre = jnp.dot(rows_in, up_weight[expert_id].T, preferred_element_type=jnp.float32) * up_scale[expert_id][None, :]
        sigmoid_gate = jax.nn.sigmoid(gate_pre)
        silu_gate = gate_pre * sigmoid_gate
        hidden = (silu_gate * up_pre).astype(jnp.bfloat16)
        full_out = jnp.dot(hidden, down_weight[expert_id], preferred_element_type=jnp.float32) * down_scale[expert_id][None, :]
        expert_out = full_out.astype(jnp.bfloat16).astype(jnp.float32)
        mixed_acc = mixed_acc.at[rows_tok].add(weight_rows[:, None] * expert_out)
        cot_rows = cotangent[rows_tok].astype(jnp.float32)
        route_rows = jnp.sum(cot_rows * expert_out, axis=1)
        route_acc = route_acc.at[safe].add(jnp.where(valid, route_rows, jnp.zeros((), jnp.float32)))
        out_grad = (cot_rows * weight_rows[:, None] * down_scale[expert_id][None, :]).astype(jnp.bfloat16)
        hidden_grad = jnp.dot(out_grad, down_weight[expert_id].T, preferred_element_type=jnp.float32)
        gate_in = (hidden_grad * up_pre * sigmoid_gate * (1.0 + gate_pre * (1.0 - sigmoid_gate)) * gate_scale[expert_id][None, :]).astype(jnp.bfloat16)
        up_in = (hidden_grad * silu_gate * up_scale[expert_id][None, :]).astype(jnp.bfloat16)
        down_g = jnp.dot(hidden.T, out_grad, preferred_element_type=jnp.float32)
        gate_g = jnp.dot(gate_in.T, rows_in, preferred_element_type=jnp.float32)
        up_g = jnp.dot(up_in.T, rows_in, preferred_element_type=jnp.float32)
        input_part = jnp.dot(gate_in, gate_weight[expert_id], preferred_element_type=jnp.float32)
        input_part = input_part + jnp.dot(up_in, up_weight[expert_id], preferred_element_type=jnp.float32)
        input_acc = input_acc.at[rows_tok].add(jnp.where(valid[:, None], input_part, jnp.zeros((), jnp.float32)))
        return (mixed_acc, input_acc, route_acc), (gate_g, up_g, down_g)

    start = (jnp.zeros((TOKENS, D), jnp.float32), jnp.zeros((TOKENS, D), jnp.float32), jnp.zeros((assigned,), jnp.float32))
    final, grads = lax.scan(one_expert, start, jnp.arange(EXPERTS, dtype=jnp.int32))
    mixed_acc, input_acc, route_acc = final
    gate_grad, up_grad, down_grad = grads
    return (mixed_acc.astype(jnp.bfloat16), input_acc.astype(jnp.bfloat16), route_acc.reshape(TOKENS, TOP), gate_grad, up_grad, down_grad)
```

```python
import jax
import jax.numpy as jnp
from jax import lax
from jax.sharding import PartitionSpec as P


def routed(
    tokens,
    route_expert,
    route_weight,
    gate_weight,
    up_weight,
    down_weight,
    gate_scale,
    up_scale,
    down_scale,
    cotangent,
):
    owners = lax.axis_size("dp")
    tok_rows, width = tokens.shape
    choose = route_expert.shape[1]
    capacity = 2 * tok_rows * choose // owners
    slots = owners * capacity
    assigned = tok_rows * choose
    col_share = width // lax.axis_size("expert")
    col_start = lax.axis_index("expert") * col_share
    flat_expert = route_expert.reshape(-1)
    one_hot = (flat_expert[:, None] == jnp.arange(owners, dtype=jnp.int32)[None, :]).astype(
        jnp.int32
    )
    order = jnp.arange(assigned, dtype=jnp.int32)
    before = (order[:, None] > order[None, :]).astype(jnp.bfloat16)
    earlier = jnp.dot(before, one_hot.astype(jnp.bfloat16), preferred_element_type=jnp.float32)
    ranks = jnp.sum(earlier.astype(jnp.int32) * one_hot, axis=1)
    slot_index = flat_expert * capacity + ranks
    slot_token = (
        jnp.zeros((slots,), jnp.int32)
        .at[slot_index]
        .set(jnp.arange(assigned, dtype=jnp.int32) // choose)
    )
    filled = jnp.zeros((slots,), jnp.bool_).at[slot_index].set(True)
    slot_weight = jnp.zeros((slots,), jnp.float32).at[slot_index].set(route_weight.reshape(-1))
    outgoing = jnp.where(
        filled[:, None], jnp.take(tokens, slot_token, axis=0), jnp.zeros((), tokens.dtype)
    )
    arrived = lax.all_to_all(
        outgoing.reshape(owners, capacity, width), "dp", split_axis=0, concat_axis=0, tiled=True
    ).reshape(slots, width)
    gate_local = gate_weight[0]
    up_local = up_weight[0]
    down_local = down_weight[0]
    gate_pre = (
        lax.dot_general(
            arrived, gate_local, (((1,), (1,)), ((), ())), preferred_element_type=jnp.float32
        )
        * gate_scale[0][None, :]
    )
    up_pre = (
        lax.dot_general(
            arrived, up_local, (((1,), (1,)), ((), ())), preferred_element_type=jnp.float32
        )
        * up_scale[0][None, :]
    )
    sigmoid_gate = jax.nn.sigmoid(gate_pre)
    silu_gate = gate_pre * sigmoid_gate
    hidden = (silu_gate * up_pre).astype(jnp.bfloat16)
    summed = lax.psum_scatter(
        lax.dot_general(
            down_local, hidden, (((0,), (1,)), ((), ())), preferred_element_type=jnp.float32
        ),
        "expert",
        scatter_dimension=0,
        tiled=True,
    )
    owner_scale = lax.dynamic_slice(down_scale, (lax.axis_index("dp"), col_start), (1, col_share))[
        0
    ]
    out_cols = (summed * owner_scale[:, None]).astype(jnp.bfloat16)
    returned = lax.all_to_all(
        out_cols.reshape(col_share, owners, capacity), "dp", split_axis=1, concat_axis=1, tiled=True
    ).reshape(col_share, slots)
    picked = (
        jnp.take(returned, slot_index, axis=1)
        .reshape(col_share, tok_rows, choose)
        .astype(jnp.float32)
    )
    mixed = jnp.sum(picked * route_weight[None, :, :], axis=2).T.astype(jnp.bfloat16)
    cot_cols = cotangent.T.astype(jnp.float32)
    route_part = jnp.sum(picked * cot_cols[:, :, None], axis=0)
    route_grad = lax.psum(route_part, "expert")
    slot_scale = jnp.repeat(down_scale, capacity, axis=0)
    cot_slots = jnp.take(cotangent, slot_token, axis=0).astype(jnp.float32)
    scale_share = lax.dynamic_slice_in_dim(slot_scale, col_start, col_share, 1)
    weighted = (cot_slots * slot_weight[:, None] * scale_share).astype(jnp.bfloat16)
    pieces = lax.all_to_all(
        weighted.reshape(owners, capacity, col_share), "dp", split_axis=0, concat_axis=0, tiled=True
    )
    out_grad = lax.all_gather(pieces, "expert", axis=2, tiled=True).reshape(slots, width)
    hidden_grad = lax.dot_general(
        out_grad, down_local, (((1,), (1,)), ((), ())), preferred_element_type=jnp.float32
    )
    gate_in = (
        hidden_grad
        * up_pre
        * sigmoid_gate
        * (1.0 + gate_pre * (1.0 - sigmoid_gate))
        * gate_scale[0][None, :]
    ).astype(jnp.bfloat16)
    up_in = (hidden_grad * silu_gate * up_scale[0][None, :]).astype(jnp.bfloat16)
    down_grad = lax.dot_general(
        hidden, out_grad, (((0,), (0,)), ((), ())), preferred_element_type=jnp.float32
    )
    gate_grad = lax.dot_general(
        gate_in, arrived, (((0,), (0,)), ((), ())), preferred_element_type=jnp.float32
    )
    up_grad = lax.dot_general(
        up_in, arrived, (((0,), (0,)), ((), ())), preferred_element_type=jnp.float32
    )
    first = lax.dot_general(
        gate_local, gate_in, (((0,), (1,)), ((), ())), preferred_element_type=jnp.float32
    )
    second = lax.dot_general(
        up_local, up_in, (((0,), (1,)), ((), ())), preferred_element_type=jnp.float32
    )
    input_cols = lax.psum_scatter(first + second, "expert", scatter_dimension=0, tiled=True)
    input_home = lax.all_to_all(
        input_cols.reshape(col_share, owners, capacity),
        "dp",
        split_axis=1,
        concat_axis=1,
        tiled=True,
    ).reshape(col_share, slots)
    token_grad = jnp.sum(
        jnp.take(input_home, slot_index, axis=1).reshape(col_share, tok_rows, choose), axis=2
    ).T.astype(jnp.bfloat16)
    return (mixed, token_grad, route_grad, gate_grad[None], up_grad[None], down_grad[None])


def dense(
    tokens,
    route_expert,
    route_weight,
    gate_weight,
    up_weight,
    down_weight,
    gate_scale,
    up_scale,
    down_scale,
    cotangent,
):
    me = lax.axis_index("dp")
    arrived = lax.all_gather(tokens, "dp", axis=0, tiled=True)
    cot_mine = lax.all_gather(cotangent, "expert", axis=1, tiled=True)
    cot_all = lax.all_gather(cot_mine, "dp", axis=0, tiled=True)
    experts = lax.all_gather(route_expert.astype(jnp.float32), "dp", axis=0, tiled=True)
    weights = lax.all_gather(route_weight, "dp", axis=0, tiled=True)
    chosen = experts == me.astype(jnp.float32)
    row_weight = jnp.sum(jnp.where(chosen, weights, 0.0), axis=1, keepdims=True)
    gate_local, up_local, down_local = gate_weight[0], up_weight[0], down_weight[0]
    scale = lax.dynamic_slice_in_dim(down_scale, me, 1, 0)
    gate_pre = (
        lax.dot_general(
            arrived, gate_local, (((1,), (1,)), ((), ())), preferred_element_type=jnp.float32
        )
        * gate_scale
    )
    up_pre = (
        lax.dot_general(
            arrived, up_local, (((1,), (1,)), ((), ())), preferred_element_type=jnp.float32
        )
        * up_scale
    )
    sigmoid_gate = jax.nn.sigmoid(gate_pre)
    silu_gate = gate_pre * sigmoid_gate
    hidden = (silu_gate * up_pre).astype(jnp.bfloat16)
    out_part = (
        lax.dot_general(
            hidden, down_local, (((1,), (0,)), ((), ())), preferred_element_type=jnp.float32
        )
        * row_weight
        * scale
    ).astype(jnp.bfloat16)
    mixed = reduce_home(out_part)
    out_grad = (cot_all.astype(jnp.float32) * row_weight * scale).astype(jnp.bfloat16)
    hidden_grad = lax.dot_general(
        out_grad, down_local, (((1,), (1,)), ((), ())), preferred_element_type=jnp.float32
    )
    gate_in = (
        hidden_grad * up_pre * sigmoid_gate * (1.0 + gate_pre * (1.0 - sigmoid_gate)) * gate_scale
    ).astype(jnp.bfloat16)
    up_in = (hidden_grad * silu_gate * up_scale).astype(jnp.bfloat16)
    input_part = (
        lax.dot_general(
            gate_in, gate_local, (((1,), (0,)), ((), ())), preferred_element_type=jnp.float32
        )
        + lax.dot_general(
            up_in, up_local, (((1,), (0,)), ((), ())), preferred_element_type=jnp.float32
        )
    ).astype(jnp.bfloat16)
    token_grad = reduce_home(input_part)
    route_row = jnp.sum(hidden.astype(jnp.float32) * hidden_grad, axis=1, keepdims=True)
    route_row = route_row / jnp.where(row_weight > 0.0, row_weight, 1.0)
    route_part = jnp.where(chosen, route_row, 0.0)
    route_sum = lax.psum(route_part, ("dp", "expert"))
    rows = tokens.shape[0]
    route_grad = lax.dynamic_slice_in_dim(route_sum, me * rows, rows, 0)
    down_grad = lax.dot_general(
        hidden, out_grad, (((0,), (0,)), ((), ())), preferred_element_type=jnp.float32
    )
    gate_grad = lax.dot_general(
        gate_in, arrived, (((0,), (0,)), ((), ())), preferred_element_type=jnp.float32
    )
    up_grad = lax.dot_general(
        up_in, arrived, (((0,), (0,)), ((), ())), preferred_element_type=jnp.float32
    )
    return (mixed, token_grad, route_grad, gate_grad[None], up_grad[None], down_grad[None])


def reduce_home(part):
    rows, width = part.shape
    owners, shares = lax.axis_size("dp"), lax.axis_size("expert")
    blocks = part.reshape(owners, rows // owners, width)
    blocks = lax.all_to_all(blocks, "dp", split_axis=0, concat_axis=0, tiled=True)
    home = jnp.sum(blocks.astype(jnp.float32), axis=0).astype(jnp.bfloat16)
    cols = home.reshape(rows // owners, shares, width // shares)
    cols = lax.all_to_all(cols, "expert", split_axis=1, concat_axis=1, tiled=True)
    return jnp.sum(cols.astype(jnp.float32), axis=1).astype(jnp.bfloat16)


def local(tokens, route_expert, *rest):
    owners = lax.axis_size("dp")
    rows, choose = route_expert.shape
    full = 2 * rows * choose >= owners * rows
    return (dense if full else routed)(tokens, route_expert, *rest)


def solution(mesh):
    return jax.shard_map(
        local,
        mesh=mesh,
        in_specs=(
            P("dp", None),
            P("dp", None),
            P("dp", None),
            P("dp", "expert", None),
            P("dp", "expert", None),
            P("dp", "expert", None),
            P("dp", "expert"),
            P("dp", "expert"),
            P(),
            P("dp", "expert"),
        ),
        out_specs=(
            P("dp", "expert"),
            P("dp", "expert"),
            P("dp", None),
            P("dp", "expert", None),
            P("dp", "expert", None),
            P("dp", "expert", None),
        ),
        check_vma=False,
    )
```

```python
import jax
import jax.numpy as jnp
from jax import lax
from jax.sharding import PartitionSpec as P


def routed(
    tokens,
    route_expert,
    route_weight,
    gate_weight,
    up_weight,
    down_weight,
    gate_scale,
    up_scale,
    down_scale,
    cotangent,
):
    owners = lax.axis_size("dp")
    tok_rows, width = tokens.shape
    choose = route_expert.shape[1]
    capacity = 2 * tok_rows * choose // owners
    slots = owners * capacity
    assigned = tok_rows * choose
    col_share = width // lax.axis_size("expert")
    col_start = lax.axis_index("expert") * col_share
    flat_expert = route_expert.reshape(-1)
    one_hot = (flat_expert[:, None] == jnp.arange(owners, dtype=jnp.int32)[None, :]).astype(
        jnp.int32
    )
    order = jnp.arange(assigned, dtype=jnp.int32)
    before = (order[:, None] > order[None, :]).astype(jnp.bfloat16)
    earlier = jnp.dot(before, one_hot.astype(jnp.bfloat16), preferred_element_type=jnp.float32)
    ranks = jnp.sum(earlier.astype(jnp.int32) * one_hot, axis=1)
    slot_index = flat_expert * capacity + ranks
    slot_token = (
        jnp.zeros((slots,), jnp.int32)
        .at[slot_index]
        .set(jnp.arange(assigned, dtype=jnp.int32) // choose)
    )
    filled = jnp.zeros((slots,), jnp.bool_).at[slot_index].set(True)
    slot_weight = jnp.zeros((slots,), jnp.float32).at[slot_index].set(route_weight.reshape(-1))
    outgoing = jnp.where(
        filled[:, None], jnp.take(tokens, slot_token, axis=0), jnp.zeros((), tokens.dtype)
    )
    arrived = lax.all_to_all(
        outgoing.reshape(owners, capacity, width), "dp", split_axis=0, concat_axis=0, tiled=True
    ).reshape(slots, width)
    gate_local = gate_weight[0]
    up_local = up_weight[0]
    down_local = down_weight[0]
    gate_pre = (
        lax.dot_general(
            arrived, gate_local, (((1,), (1,)), ((), ())), preferred_element_type=jnp.float32
        )
        * gate_scale[0][None, :]
    )
    up_pre = (
        lax.dot_general(
            arrived, up_local, (((1,), (1,)), ((), ())), preferred_element_type=jnp.float32
        )
        * up_scale[0][None, :]
    )
    sigmoid_gate = jax.nn.sigmoid(gate_pre)
    silu_gate = gate_pre * sigmoid_gate
    hidden = (silu_gate * up_pre).astype(jnp.bfloat16)
    summed = lax.psum_scatter(
        lax.dot_general(
            down_local, hidden, (((0,), (1,)), ((), ())), preferred_element_type=jnp.float32
        ),
        "expert",
        scatter_dimension=0,
        tiled=True,
    )
    owner_scale = lax.dynamic_slice(down_scale, (lax.axis_index("dp"), col_start), (1, col_share))[
        0
    ]
    out_cols = (summed * owner_scale[:, None]).astype(jnp.bfloat16)
    returned = lax.all_to_all(
        out_cols.reshape(col_share, owners, capacity), "dp", split_axis=1, concat_axis=1, tiled=True
    ).reshape(col_share, slots)
    picked = (
        jnp.take(returned, slot_index, axis=1)
        .reshape(col_share, tok_rows, choose)
        .astype(jnp.float32)
    )
    mixed = jnp.sum(picked * route_weight[None, :, :], axis=2).T.astype(jnp.bfloat16)
    cot_cols = cotangent.T.astype(jnp.float32)
    route_part = jnp.sum(picked * cot_cols[:, :, None], axis=0)
    route_grad = lax.psum(route_part, "expert")
    slot_scale = jnp.repeat(down_scale, capacity, axis=0)
    cot_slots = jnp.take(cotangent, slot_token, axis=0).astype(jnp.float32)
    scale_share = lax.dynamic_slice_in_dim(slot_scale, col_start, col_share, 1)
    weighted = (cot_slots * slot_weight[:, None] * scale_share).astype(jnp.bfloat16)
    pieces = lax.all_to_all(
        weighted.reshape(owners, capacity, col_share), "dp", split_axis=0, concat_axis=0, tiled=True
    )
    out_grad = lax.all_gather(pieces, "expert", axis=2, tiled=True).reshape(slots, width)
    hidden_grad = lax.dot_general(
        out_grad, down_local, (((1,), (1,)), ((), ())), preferred_element_type=jnp.float32
    )
    gate_in = (
        hidden_grad
        * up_pre
        * sigmoid_gate
        * (1.0 + gate_pre * (1.0 - sigmoid_gate))
        * gate_scale[0][None, :]
    ).astype(jnp.bfloat16)
    up_in = (hidden_grad * silu_gate * up_scale[0][None, :]).astype(jnp.bfloat16)
    down_grad = lax.dot_general(
        hidden, out_grad, (((0,), (0,)), ((), ())), preferred_element_type=jnp.float32
    )
    gate_grad = lax.dot_general(
        gate_in, arrived, (((0,), (0,)), ((), ())), preferred_element_type=jnp.float32
    )
    up_grad = lax.dot_general(
        up_in, arrived, (((0,), (0,)), ((), ())), preferred_element_type=jnp.float32
    )
    first = lax.dot_general(
        gate_local, gate_in, (((0,), (1,)), ((), ())), preferred_element_type=jnp.float32
    )
    second = lax.dot_general(
        up_local, up_in, (((0,), (1,)), ((), ())), preferred_element_type=jnp.float32
    )
    input_cols = lax.psum_scatter(first + second, "expert", scatter_dimension=0, tiled=True)
    input_home = lax.all_to_all(
        input_cols.reshape(col_share, owners, capacity),
        "dp",
        split_axis=1,
        concat_axis=1,
        tiled=True,
    ).reshape(col_share, slots)
    token_grad = jnp.sum(
        jnp.take(input_home, slot_index, axis=1).reshape(col_share, tok_rows, choose), axis=2
    ).T.astype(jnp.bfloat16)
    return (mixed, token_grad, route_grad, gate_grad[None], up_grad[None], down_grad[None])


def dense(
    tokens,
    route_expert,
    route_weight,
    gate_weight,
    up_weight,
    down_weight,
    gate_scale,
    up_scale,
    down_scale,
    cotangent,
):
    me = lax.axis_index("dp")
    choose = route_expert.shape[1]
    routes = jnp.concatenate([route_expert.astype(jnp.float32), route_weight], axis=1)
    arrived = gather_tokens(tokens)
    routes = lax.all_gather(routes, "dp", axis=0, tiled=True)
    cot_all = gather_tokens(gather_columns(cotangent))
    experts, weights = routes[:, :choose], routes[:, choose:]
    chosen = experts == me.astype(jnp.float32)
    row_weight = jnp.sum(jnp.where(chosen, weights, 0.0), axis=1, keepdims=True)
    gate_local, up_local, down_local = gate_weight[0], up_weight[0], down_weight[0]
    scale = lax.dynamic_slice_in_dim(down_scale, me, 1, 0)
    gate_pre = (
        lax.dot_general(
            arrived, gate_local, (((1,), (1,)), ((), ())), preferred_element_type=jnp.float32
        )
        * gate_scale
    )
    up_pre = (
        lax.dot_general(
            arrived, up_local, (((1,), (1,)), ((), ())), preferred_element_type=jnp.float32
        )
        * up_scale
    )
    sigmoid_gate = jax.nn.sigmoid(gate_pre)
    silu_gate = gate_pre * sigmoid_gate
    hidden = (silu_gate * up_pre).astype(jnp.bfloat16)
    out_part = (
        lax.dot_general(
            hidden, down_local, (((1,), (0,)), ((), ())), preferred_element_type=jnp.float32
        )
        * row_weight
        * scale
    ).astype(jnp.bfloat16)
    mixed = reduce_home(out_part)
    out_grad = (cot_all.astype(jnp.float32) * row_weight * scale).astype(jnp.bfloat16)
    hidden_grad = lax.dot_general(
        out_grad, down_local, (((1,), (1,)), ((), ())), preferred_element_type=jnp.float32
    )
    gate_in = (
        hidden_grad * up_pre * sigmoid_gate * (1.0 + gate_pre * (1.0 - sigmoid_gate)) * gate_scale
    ).astype(jnp.bfloat16)
    up_in = (hidden_grad * silu_gate * up_scale).astype(jnp.bfloat16)
    input_part = (
        lax.dot_general(
            gate_in, gate_local, (((1,), (0,)), ((), ())), preferred_element_type=jnp.float32
        )
        + lax.dot_general(
            up_in, up_local, (((1,), (0,)), ((), ())), preferred_element_type=jnp.float32
        )
    ).astype(jnp.bfloat16)
    token_grad = reduce_home(input_part)
    route_row = jnp.sum(hidden.astype(jnp.float32) * hidden_grad, axis=1, keepdims=True)
    route_row = route_row / jnp.where(row_weight > 0.0, row_weight, 1.0)
    route_part = jnp.where(chosen, route_row, 0.0)
    route_grad = sum_shares(sum_tokens(route_part.reshape(-1, tokens.shape[0], choose)))
    down_grad = lax.dot_general(
        hidden, out_grad, (((0,), (0,)), ((), ())), preferred_element_type=jnp.float32
    )
    gate_grad = lax.dot_general(
        gate_in, arrived, (((0,), (0,)), ((), ())), preferred_element_type=jnp.float32
    )
    up_grad = lax.dot_general(
        up_in, arrived, (((0,), (0,)), ((), ())), preferred_element_type=jnp.float32
    )
    return (mixed, token_grad, route_grad, gate_grad[None], up_grad[None], down_grad[None])


def swap(block, bit):
    owners = lax.axis_size("dp")
    return lax.ppermute(block, "dp", [(i, i ^ bit) for i in range(owners)])


def bits():
    owners = lax.axis_size("dp")
    return [1 << i for i in range(owners.bit_length() - 1)]


def orders():
    upper = bits()[1:]
    return (upper, upper[::-1])


def in_order(block, bit):
    other = swap(block, bit)
    first = (lax.axis_index("dp") & bit) == 0
    return jnp.where(first, block, other), jnp.where(first, other, block)


def gather_tokens(mine):
    rows, width = mine.shape
    upper = bits()[1:]
    halves = []
    for order, half in zip(orders(), jnp.split(mine, 2, axis=1)):
        block = half.reshape((1,) * len(upper) + half.shape)
        for bit in order:
            axis = len(upper) - 1 - upper.index(bit)
            block = jnp.concatenate(in_order(block, bit), axis=axis)
        halves.append(block.reshape(-1, rows, width // 2))
    both = [jnp.stack(in_order(half, bits()[0]), axis=1) for half in halves]
    return jnp.concatenate(both, axis=-1).reshape(-1, width)


def shift(block, by):
    shares = lax.axis_size("expert")
    return lax.ppermute(block, "expert", [(i, (i + by) % shares) for i in range(shares)])


def gather_columns(mine):
    shares, me = lax.axis_size("expert"), lax.axis_index("expert")
    width = mine.shape[1]
    out = jnp.zeros((mine.shape[0], shares * width), mine.dtype)
    for by in range(shares):
        block = mine if by == 0 else shift(mine, by)
        source = lax.rem(me - by + shares, shares)
        out = lax.dynamic_update_slice_in_dim(out, block, source * width, 1)
    return out


def sum_shares(mine):
    return sum([shift(mine, by) for by in range(1, lax.axis_size("expert"))], mine)


def add_wide(a, b):
    return (a.astype(jnp.float32) + b.astype(jnp.float32)).astype(a.dtype)


def halve(block, axis, bit):
    own = (lax.axis_index("dp") & bit) // bit
    keep = lax.dynamic_index_in_dim(block, own, axis, keepdims=True)
    give = lax.dynamic_index_in_dim(block, 1 - own, axis, keepdims=True)
    return add_wide(keep, swap(give, bit))


def sum_tokens(blocks):
    count = len(bits())
    shape = blocks.shape[1:]
    block = blocks.reshape((2,) * count + shape)
    block = halve(block, count - 1, bits()[0])
    parts = jnp.split(block, 2, axis=-1)
    done = []
    for order, part in zip(orders(), parts):
        for bit in order:
            part = halve(part, count - 1 - bits().index(bit), bit)
        done.append(part.reshape(shape[0], -1))
    return jnp.concatenate(done, axis=1)


def reduce_home(part):
    owners, shares = lax.axis_size("dp"), lax.axis_size("expert")
    home = sum_tokens(part.reshape(owners, -1, part.shape[1]))
    me = lax.axis_index("expert")
    width = part.shape[1] // shares
    total = lax.dynamic_slice_in_dim(home, me * width, width, 1).astype(jnp.float32)
    for by in range(1, shares):
        target = lax.rem(me + by, shares)
        sent = lax.dynamic_slice_in_dim(home, target * width, width, 1)
        total = total + shift(sent, by).astype(jnp.float32)
    return total.astype(jnp.bfloat16)


def local(tokens, route_expert, *rest):
    owners = lax.axis_size("dp")
    rows, choose = route_expert.shape
    full = 2 * rows * choose >= owners * rows and owners & (owners - 1) == 0
    return (dense if full else routed)(tokens, route_expert, *rest)


def solution(mesh):
    return jax.shard_map(
        local,
        mesh=mesh,
        in_specs=(
            P("dp", None),
            P("dp", None),
            P("dp", None),
            P("dp", "expert", None),
            P("dp", "expert", None),
            P("dp", "expert", None),
            P("dp", "expert"),
            P("dp", "expert"),
            P(),
            P("dp", "expert"),
        ),
        out_specs=(
            P("dp", "expert"),
            P("dp", "expert"),
            P("dp", None),
            P("dp", "expert", None),
            P("dp", "expert", None),
            P("dp", "expert", None),
        ),
        check_vma=False,
    )
```

```python
import jax
import jax.numpy as jnp
from jax import lax
from jax.sharding import PartitionSpec as P


def routed(
    tokens,
    route_expert,
    route_weight,
    gate_weight,
    up_weight,
    down_weight,
    gate_scale,
    up_scale,
    down_scale,
    cotangent,
):
    owners = lax.axis_size("dp")
    tok_rows, width = tokens.shape
    choose = route_expert.shape[1]
    capacity = 2 * tok_rows * choose // owners
    slots = owners * capacity
    assigned = tok_rows * choose
    col_share = width // lax.axis_size("expert")
    col_start = lax.axis_index("expert") * col_share
    flat_expert = route_expert.reshape(-1)
    one_hot = (flat_expert[:, None] == jnp.arange(owners, dtype=jnp.int32)[None, :]).astype(
        jnp.int32
    )
    order = jnp.arange(assigned, dtype=jnp.int32)
    before = (order[:, None] > order[None, :]).astype(jnp.bfloat16)
    earlier = jnp.dot(before, one_hot.astype(jnp.bfloat16), preferred_element_type=jnp.float32)
    ranks = jnp.sum(earlier.astype(jnp.int32) * one_hot, axis=1)
    slot_index = flat_expert * capacity + ranks
    slot_token = (
        jnp.zeros((slots,), jnp.int32)
        .at[slot_index]
        .set(jnp.arange(assigned, dtype=jnp.int32) // choose)
    )
    filled = jnp.zeros((slots,), jnp.bool_).at[slot_index].set(True)
    slot_weight = jnp.zeros((slots,), jnp.float32).at[slot_index].set(route_weight.reshape(-1))
    outgoing = jnp.where(
        filled[:, None], jnp.take(tokens, slot_token, axis=0), jnp.zeros((), tokens.dtype)
    )
    arrived = lax.all_to_all(
        outgoing.reshape(owners, capacity, width), "dp", split_axis=0, concat_axis=0, tiled=True
    ).reshape(slots, width)
    gate_local = gate_weight[0]
    up_local = up_weight[0]
    down_local = down_weight[0]
    gate_pre = (
        lax.dot_general(
            arrived, gate_local, (((1,), (1,)), ((), ())), preferred_element_type=jnp.float32
        )
        * gate_scale[0][None, :]
    )
    up_pre = (
        lax.dot_general(
            arrived, up_local, (((1,), (1,)), ((), ())), preferred_element_type=jnp.float32
        )
        * up_scale[0][None, :]
    )
    sigmoid_gate = jax.nn.sigmoid(gate_pre)
    silu_gate = gate_pre * sigmoid_gate
    hidden = (silu_gate * up_pre).astype(jnp.bfloat16)
    summed = lax.psum_scatter(
        lax.dot_general(
            down_local, hidden, (((0,), (1,)), ((), ())), preferred_element_type=jnp.float32
        ),
        "expert",
        scatter_dimension=0,
        tiled=True,
    )
    owner_scale = lax.dynamic_slice(down_scale, (lax.axis_index("dp"), col_start), (1, col_share))[
        0
    ]
    out_cols = (summed * owner_scale[:, None]).astype(jnp.bfloat16)
    returned = lax.all_to_all(
        out_cols.reshape(col_share, owners, capacity), "dp", split_axis=1, concat_axis=1, tiled=True
    ).reshape(col_share, slots)
    picked = (
        jnp.take(returned, slot_index, axis=1)
        .reshape(col_share, tok_rows, choose)
        .astype(jnp.float32)
    )
    mixed = jnp.sum(picked * route_weight[None, :, :], axis=2).T.astype(jnp.bfloat16)
    cot_cols = cotangent.T.astype(jnp.float32)
    route_part = jnp.sum(picked * cot_cols[:, :, None], axis=0)
    route_grad = lax.psum(route_part, "expert")
    slot_scale = jnp.repeat(down_scale, capacity, axis=0)
    cot_slots = jnp.take(cotangent, slot_token, axis=0).astype(jnp.float32)
    scale_share = lax.dynamic_slice_in_dim(slot_scale, col_start, col_share, 1)
    weighted = (cot_slots * slot_weight[:, None] * scale_share).astype(jnp.bfloat16)
    pieces = lax.all_to_all(
        weighted.reshape(owners, capacity, col_share), "dp", split_axis=0, concat_axis=0, tiled=True
    )
    out_grad = lax.all_gather(pieces, "expert", axis=2, tiled=True).reshape(slots, width)
    hidden_grad = lax.dot_general(
        out_grad, down_local, (((1,), (1,)), ((), ())), preferred_element_type=jnp.float32
    )
    gate_in = (
        hidden_grad
        * up_pre
        * sigmoid_gate
        * (1.0 + gate_pre * (1.0 - sigmoid_gate))
        * gate_scale[0][None, :]
    ).astype(jnp.bfloat16)
    up_in = (hidden_grad * silu_gate * up_scale[0][None, :]).astype(jnp.bfloat16)
    down_grad = lax.dot_general(
        hidden, out_grad, (((0,), (0,)), ((), ())), preferred_element_type=jnp.float32
    )
    gate_grad = lax.dot_general(
        gate_in, arrived, (((0,), (0,)), ((), ())), preferred_element_type=jnp.float32
    )
    up_grad = lax.dot_general(
        up_in, arrived, (((0,), (0,)), ((), ())), preferred_element_type=jnp.float32
    )
    first = lax.dot_general(
        gate_local, gate_in, (((0,), (1,)), ((), ())), preferred_element_type=jnp.float32
    )
    second = lax.dot_general(
        up_local, up_in, (((0,), (1,)), ((), ())), preferred_element_type=jnp.float32
    )
    input_cols = lax.psum_scatter(first + second, "expert", scatter_dimension=0, tiled=True)
    input_home = lax.all_to_all(
        input_cols.reshape(col_share, owners, capacity),
        "dp",
        split_axis=1,
        concat_axis=1,
        tiled=True,
    ).reshape(col_share, slots)
    token_grad = jnp.sum(
        jnp.take(input_home, slot_index, axis=1).reshape(col_share, tok_rows, choose), axis=2
    ).T.astype(jnp.bfloat16)
    return (mixed, token_grad, route_grad, gate_grad[None], up_grad[None], down_grad[None])


def dense(
    tokens,
    route_expert,
    route_weight,
    gate_weight,
    up_weight,
    down_weight,
    gate_scale,
    up_scale,
    down_scale,
    cotangent,
):
    me = lax.axis_index("dp")
    choose = route_expert.shape[1]
    routes = jnp.concatenate([route_expert.astype(jnp.float32), route_weight], axis=1)
    arrived = gather_tokens(tokens)
    routes = gather_small(routes.T[None]).swapaxes(1, 2).reshape(-1, 2 * choose)
    cot_all = gather_tokens(gather_columns(cotangent))
    experts, weights = routes[:, :choose], routes[:, choose:]
    chosen = experts == me.astype(jnp.float32)
    row_weight = jnp.sum(jnp.where(chosen, weights, 0.0), axis=1, keepdims=True)
    gate_local, up_local, down_local = gate_weight[0], up_weight[0], down_weight[0]
    scale = lax.dynamic_slice_in_dim(down_scale, me, 1, 0)
    gate_pre = (
        lax.dot_general(
            arrived, gate_local, (((1,), (1,)), ((), ())), preferred_element_type=jnp.float32
        )
        * gate_scale
    )
    up_pre = (
        lax.dot_general(
            arrived, up_local, (((1,), (1,)), ((), ())), preferred_element_type=jnp.float32
        )
        * up_scale
    )
    sigmoid_gate = jax.nn.sigmoid(gate_pre)
    silu_gate = gate_pre * sigmoid_gate
    hidden = (silu_gate * up_pre).astype(jnp.bfloat16)
    out_part = (
        lax.dot_general(
            hidden, down_local, (((1,), (0,)), ((), ())), preferred_element_type=jnp.float32
        )
        * row_weight
        * scale
    ).astype(jnp.bfloat16)
    mixed = reduce_home(out_part)
    out_grad = (cot_all.astype(jnp.float32) * row_weight * scale).astype(jnp.bfloat16)
    hidden_grad = lax.dot_general(
        out_grad, down_local, (((1,), (1,)), ((), ())), preferred_element_type=jnp.float32
    )
    gate_in = (
        hidden_grad * up_pre * sigmoid_gate * (1.0 + gate_pre * (1.0 - sigmoid_gate)) * gate_scale
    ).astype(jnp.bfloat16)
    up_in = (hidden_grad * silu_gate * up_scale).astype(jnp.bfloat16)
    input_part = (
        lax.dot_general(
            gate_in, gate_local, (((1,), (0,)), ((), ())), preferred_element_type=jnp.float32
        )
        + lax.dot_general(
            up_in, up_local, (((1,), (0,)), ((), ())), preferred_element_type=jnp.float32
        )
    ).astype(jnp.bfloat16)
    token_grad = reduce_home(input_part)
    route_row = jnp.sum(hidden.astype(jnp.float32) * hidden_grad, axis=1, keepdims=True)
    route_row = route_row / jnp.where(row_weight > 0.0, row_weight, 1.0)
    route_part = jnp.where(chosen, route_row, 0.0)
    route_grad = sum_shares(sum_tokens(route_part.reshape(-1, tokens.shape[0], choose)))
    down_grad = lax.dot_general(
        hidden, out_grad, (((0,), (0,)), ((), ())), preferred_element_type=jnp.float32
    )
    gate_grad = lax.dot_general(
        gate_in, arrived, (((0,), (0,)), ((), ())), preferred_element_type=jnp.float32
    )
    up_grad = lax.dot_general(
        up_in, arrived, (((0,), (0,)), ((), ())), preferred_element_type=jnp.float32
    )
    return (mixed, token_grad, route_grad, gate_grad[None], up_grad[None], down_grad[None])


def swap(block, bit):
    owners = lax.axis_size("dp")
    return lax.ppermute(block, "dp", [(i, i ^ bit) for i in range(owners)])


def bits():
    owners = lax.axis_size("dp")
    return [1 << i for i in range(owners.bit_length() - 1)]


def orders():
    upper = bits()[1:]
    return (upper, upper[::-1])


def in_order(block, bit):
    other = swap(block, bit)
    first = (lax.axis_index("dp") & bit) == 0
    return jnp.where(first, block, other), jnp.where(first, other, block)


def gather_tokens(mine):
    rows, width = mine.shape
    upper = bits()[1:]
    halves = []
    for order, half in zip(orders(), jnp.split(mine, 2, axis=1)):
        block = half.reshape((1,) * len(upper) + half.shape)
        for bit in order:
            axis = len(upper) - 1 - upper.index(bit)
            block = jnp.concatenate(in_order(block, bit), axis=axis)
        halves.append(block.reshape(-1, rows, width // 2))
    both = [jnp.stack(in_order(half, bits()[0]), axis=1) for half in halves]
    return jnp.concatenate(both, axis=-1).reshape(-1, width)


def gather_small(block):
    for bit in bits():
        block = jnp.concatenate(in_order(block, bit), axis=0)
    return block


def shift(block, by):
    shares = lax.axis_size("expert")
    return lax.ppermute(block, "expert", [(i, (i + by) % shares) for i in range(shares)])


def gather_columns(mine):
    shares, me = lax.axis_size("expert"), lax.axis_index("expert")
    width = mine.shape[1]
    out = jnp.zeros((mine.shape[0], shares * width), mine.dtype)
    for by in range(shares):
        block = mine if by == 0 else shift(mine, by)
        source = lax.rem(me - by + shares, shares)
        out = lax.dynamic_update_slice_in_dim(out, block, source * width, 1)
    return out


def sum_shares(mine):
    return sum([shift(mine, by) for by in range(1, lax.axis_size("expert"))], mine)


def add_wide(a, b):
    return (a.astype(jnp.float32) + b.astype(jnp.float32)).astype(a.dtype)


def halve(block, axis, bit):
    own = (lax.axis_index("dp") & bit) // bit
    keep = lax.dynamic_index_in_dim(block, own, axis, keepdims=True)
    give = lax.dynamic_index_in_dim(block, 1 - own, axis, keepdims=True)
    return add_wide(keep, swap(give, bit))


def sum_tokens(blocks):
    count = len(bits())
    shape = blocks.shape[1:]
    block = blocks.reshape((2,) * count + shape)
    block = halve(block, count - 1, bits()[0])
    parts = jnp.split(block, 2, axis=-1)
    done = []
    for order, part in zip(orders(), parts):
        for bit in order:
            part = halve(part, count - 1 - bits().index(bit), bit)
        done.append(part.reshape(shape[0], -1))
    return jnp.concatenate(done, axis=1)


def reduce_home(part):
    owners, shares = lax.axis_size("dp"), lax.axis_size("expert")
    home = sum_tokens(part.reshape(owners, -1, part.shape[1]))
    me = lax.axis_index("expert")
    width = part.shape[1] // shares
    total = lax.dynamic_slice_in_dim(home, me * width, width, 1).astype(jnp.float32)
    for by in range(1, shares):
        target = lax.rem(me + by, shares)
        sent = lax.dynamic_slice_in_dim(home, target * width, width, 1)
        total = total + shift(sent, by).astype(jnp.float32)
    return total.astype(jnp.bfloat16)


def local(tokens, route_expert, *rest):
    owners = lax.axis_size("dp")
    rows, choose = route_expert.shape
    full = 2 * rows * choose >= owners * rows and owners & (owners - 1) == 0
    return (dense if full else routed)(tokens, route_expert, *rest)


def solution(mesh):
    return jax.shard_map(
        local,
        mesh=mesh,
        in_specs=(
            P("dp", None),
            P("dp", None),
            P("dp", None),
            P("dp", "expert", None),
            P("dp", "expert", None),
            P("dp", "expert", None),
            P("dp", "expert"),
            P("dp", "expert"),
            P(),
            P("dp", "expert"),
        ),
        out_specs=(
            P("dp", "expert"),
            P("dp", "expert"),
            P("dp", None),
            P("dp", "expert", None),
            P("dp", "expert", None),
            P("dp", "expert", None),
        ),
        check_vma=False,
    )
```

```python
import jax
import jax.numpy as jnp
from jax import lax
from jax.sharding import PartitionSpec as P


def routed(
    tokens,
    route_expert,
    route_weight,
    gate_weight,
    up_weight,
    down_weight,
    gate_scale,
    up_scale,
    down_scale,
    cotangent,
):
    owners = lax.axis_size("dp")
    tok_rows, width = tokens.shape
    choose = route_expert.shape[1]
    capacity = 2 * tok_rows * choose // owners
    slots = owners * capacity
    assigned = tok_rows * choose
    col_share = width // lax.axis_size("expert")
    col_start = lax.axis_index("expert") * col_share
    flat_expert = route_expert.reshape(-1)
    one_hot = (flat_expert[:, None] == jnp.arange(owners, dtype=jnp.int32)[None, :]).astype(
        jnp.int32
    )
    order = jnp.arange(assigned, dtype=jnp.int32)
    before = (order[:, None] > order[None, :]).astype(jnp.bfloat16)
    earlier = jnp.dot(before, one_hot.astype(jnp.bfloat16), preferred_element_type=jnp.float32)
    ranks = jnp.sum(earlier.astype(jnp.int32) * one_hot, axis=1)
    slot_index = flat_expert * capacity + ranks
    slot_token = (
        jnp.zeros((slots,), jnp.int32)
        .at[slot_index]
        .set(jnp.arange(assigned, dtype=jnp.int32) // choose)
    )
    filled = jnp.zeros((slots,), jnp.bool_).at[slot_index].set(True)
    slot_weight = jnp.zeros((slots,), jnp.float32).at[slot_index].set(route_weight.reshape(-1))
    outgoing = jnp.where(
        filled[:, None], jnp.take(tokens, slot_token, axis=0), jnp.zeros((), tokens.dtype)
    )
    arrived = lax.all_to_all(
        outgoing.reshape(owners, capacity, width), "dp", split_axis=0, concat_axis=0, tiled=True
    ).reshape(slots, width)
    gate_local = gate_weight[0]
    up_local = up_weight[0]
    down_local = down_weight[0]
    gate_pre = (
        lax.dot_general(
            arrived, gate_local, (((1,), (1,)), ((), ())), preferred_element_type=jnp.float32
        )
        * gate_scale[0][None, :]
    )
    up_pre = (
        lax.dot_general(
            arrived, up_local, (((1,), (1,)), ((), ())), preferred_element_type=jnp.float32
        )
        * up_scale[0][None, :]
    )
    sigmoid_gate = jax.nn.sigmoid(gate_pre)
    silu_gate = gate_pre * sigmoid_gate
    hidden = (silu_gate * up_pre).astype(jnp.bfloat16)
    summed = lax.psum_scatter(
        lax.dot_general(
            down_local, hidden, (((0,), (1,)), ((), ())), preferred_element_type=jnp.float32
        ),
        "expert",
        scatter_dimension=0,
        tiled=True,
    )
    owner_scale = lax.dynamic_slice(down_scale, (lax.axis_index("dp"), col_start), (1, col_share))[
        0
    ]
    out_cols = (summed * owner_scale[:, None]).astype(jnp.bfloat16)
    returned = lax.all_to_all(
        out_cols.reshape(col_share, owners, capacity), "dp", split_axis=1, concat_axis=1, tiled=True
    ).reshape(col_share, slots)
    picked = (
        jnp.take(returned, slot_index, axis=1)
        .reshape(col_share, tok_rows, choose)
        .astype(jnp.float32)
    )
    mixed = jnp.sum(picked * route_weight[None, :, :], axis=2).T.astype(jnp.bfloat16)
    cot_cols = cotangent.T.astype(jnp.float32)
    route_part = jnp.sum(picked * cot_cols[:, :, None], axis=0)
    route_grad = lax.psum(route_part, "expert")
    slot_scale = jnp.repeat(down_scale, capacity, axis=0)
    cot_slots = jnp.take(cotangent, slot_token, axis=0).astype(jnp.float32)
    scale_share = lax.dynamic_slice_in_dim(slot_scale, col_start, col_share, 1)
    weighted = (cot_slots * slot_weight[:, None] * scale_share).astype(jnp.bfloat16)
    pieces = lax.all_to_all(
        weighted.reshape(owners, capacity, col_share), "dp", split_axis=0, concat_axis=0, tiled=True
    )
    out_grad = lax.all_gather(pieces, "expert", axis=2, tiled=True).reshape(slots, width)
    hidden_grad = lax.dot_general(
        out_grad, down_local, (((1,), (1,)), ((), ())), preferred_element_type=jnp.float32
    )
    gate_in = (
        hidden_grad
        * up_pre
        * sigmoid_gate
        * (1.0 + gate_pre * (1.0 - sigmoid_gate))
        * gate_scale[0][None, :]
    ).astype(jnp.bfloat16)
    up_in = (hidden_grad * silu_gate * up_scale[0][None, :]).astype(jnp.bfloat16)
    down_grad = lax.dot_general(
        hidden, out_grad, (((0,), (0,)), ((), ())), preferred_element_type=jnp.float32
    )
    gate_grad = lax.dot_general(
        gate_in, arrived, (((0,), (0,)), ((), ())), preferred_element_type=jnp.float32
    )
    up_grad = lax.dot_general(
        up_in, arrived, (((0,), (0,)), ((), ())), preferred_element_type=jnp.float32
    )
    first = lax.dot_general(
        gate_local, gate_in, (((0,), (1,)), ((), ())), preferred_element_type=jnp.float32
    )
    second = lax.dot_general(
        up_local, up_in, (((0,), (1,)), ((), ())), preferred_element_type=jnp.float32
    )
    input_cols = lax.psum_scatter(first + second, "expert", scatter_dimension=0, tiled=True)
    input_home = lax.all_to_all(
        input_cols.reshape(col_share, owners, capacity),
        "dp",
        split_axis=1,
        concat_axis=1,
        tiled=True,
    ).reshape(col_share, slots)
    token_grad = jnp.sum(
        jnp.take(input_home, slot_index, axis=1).reshape(col_share, tok_rows, choose), axis=2
    ).T.astype(jnp.bfloat16)
    return (mixed, token_grad, route_grad, gate_grad[None], up_grad[None], down_grad[None])


def dense(
    tokens,
    route_expert,
    route_weight,
    gate_weight,
    up_weight,
    down_weight,
    gate_scale,
    up_scale,
    down_scale,
    cotangent,
):
    me = lax.axis_index("dp")
    choose = route_expert.shape[1]
    routes = jnp.concatenate([route_expert.astype(jnp.float32), route_weight], axis=1)
    halves = gather_chips(tokens)
    cot_mine, halves = lax.optimization_barrier((gather_columns(cotangent), halves))
    arrived = gather_pair(halves)
    routes = gather_small(routes.T[None]).swapaxes(1, 2).reshape(-1, 2 * choose)
    cot_all = gather_pair(gather_chips(cot_mine))
    experts, weights = routes[:, :choose], routes[:, choose:]
    chosen = experts == me.astype(jnp.float32)
    row_weight = jnp.sum(jnp.where(chosen, weights, 0.0), axis=1, keepdims=True)
    gate_local, up_local, down_local = gate_weight[0], up_weight[0], down_weight[0]
    scale = lax.dynamic_slice_in_dim(down_scale, me, 1, 0)
    gate_pre = (
        lax.dot_general(
            arrived, gate_local, (((1,), (1,)), ((), ())), preferred_element_type=jnp.float32
        )
        * gate_scale
    )
    up_pre = (
        lax.dot_general(
            arrived, up_local, (((1,), (1,)), ((), ())), preferred_element_type=jnp.float32
        )
        * up_scale
    )
    sigmoid_gate = jax.nn.sigmoid(gate_pre)
    silu_gate = gate_pre * sigmoid_gate
    hidden = (silu_gate * up_pre).astype(jnp.bfloat16)
    out_part = (
        lax.dot_general(
            hidden, down_local, (((1,), (0,)), ((), ())), preferred_element_type=jnp.float32
        )
        * row_weight
        * scale
    ).astype(jnp.bfloat16)
    mixed = reduce_home(out_part)
    out_grad = (cot_all.astype(jnp.float32) * row_weight * scale).astype(jnp.bfloat16)
    hidden_grad = lax.dot_general(
        out_grad, down_local, (((1,), (1,)), ((), ())), preferred_element_type=jnp.float32
    )
    gate_in = (
        hidden_grad * up_pre * sigmoid_gate * (1.0 + gate_pre * (1.0 - sigmoid_gate)) * gate_scale
    ).astype(jnp.bfloat16)
    up_in = (hidden_grad * silu_gate * up_scale).astype(jnp.bfloat16)
    input_part = (
        lax.dot_general(
            gate_in, gate_local, (((1,), (0,)), ((), ())), preferred_element_type=jnp.float32
        )
        + lax.dot_general(
            up_in, up_local, (((1,), (0,)), ((), ())), preferred_element_type=jnp.float32
        )
    ).astype(jnp.bfloat16)
    input_part, gate_late, up_late, hidden_late = lax.optimization_barrier(
        (input_part, gate_in, up_in, hidden)
    )
    token_grad = reduce_home(input_part)
    route_row = jnp.sum(hidden.astype(jnp.float32) * hidden_grad, axis=1, keepdims=True)
    route_row = route_row / jnp.where(row_weight > 0.0, row_weight, 1.0)
    route_part = jnp.where(chosen, route_row, 0.0)
    route_grad = sum_shares(sum_tokens(route_part.reshape(-1, tokens.shape[0], choose)))
    down_grad = lax.dot_general(
        hidden_late, out_grad, (((0,), (0,)), ((), ())), preferred_element_type=jnp.float32
    )
    gate_grad = lax.dot_general(
        gate_late, arrived, (((0,), (0,)), ((), ())), preferred_element_type=jnp.float32
    )
    up_grad = lax.dot_general(
        up_late, arrived, (((0,), (0,)), ((), ())), preferred_element_type=jnp.float32
    )
    return (mixed, token_grad, route_grad, gate_grad[None], up_grad[None], down_grad[None])


def swap(block, bit):
    owners = lax.axis_size("dp")
    return lax.ppermute(block, "dp", [(i, i ^ bit) for i in range(owners)])


def bits():
    owners = lax.axis_size("dp")
    return [1 << i for i in range(owners.bit_length() - 1)]


def orders():
    upper = bits()[1:]
    return (upper, upper[::-1])


def in_order(block, bit):
    other = swap(block, bit)
    first = (lax.axis_index("dp") & bit) == 0
    return jnp.where(first, block, other), jnp.where(first, other, block)


def gather_chips(mine):
    rows, width = mine.shape
    upper = bits()[1:]
    halves = []
    for order, half in zip(orders(), jnp.split(mine, 2, axis=1)):
        block = half.reshape((1,) * len(upper) + half.shape)
        for bit in order:
            axis = len(upper) - 1 - upper.index(bit)
            block = jnp.concatenate(in_order(block, bit), axis=axis)
        halves.append(block.reshape(-1, rows, width // 2))
    return halves


def gather_pair(halves):
    both = [jnp.stack(in_order(half, bits()[0]), axis=1) for half in halves]
    return jnp.concatenate(both, axis=-1).reshape(-1, 2 * halves[0].shape[-1])


def gather_small(block):
    for bit in bits():
        block = jnp.concatenate(in_order(block, bit), axis=0)
    return block


def shift(block, by):
    shares = lax.axis_size("expert")
    return lax.ppermute(block, "expert", [(i, (i + by) % shares) for i in range(shares)])


def gather_columns(mine):
    shares, me = lax.axis_size("expert"), lax.axis_index("expert")
    width = mine.shape[1]
    out = jnp.zeros((mine.shape[0], shares * width), mine.dtype)
    for by in range(shares):
        block = mine if by == 0 else shift(mine, by)
        source = lax.rem(me - by + shares, shares)
        out = lax.dynamic_update_slice_in_dim(out, block, source * width, 1)
    return out


def sum_shares(mine):
    return sum([shift(mine, by) for by in range(1, lax.axis_size("expert"))], mine)


def add_wide(a, b):
    return (a.astype(jnp.float32) + b.astype(jnp.float32)).astype(a.dtype)


def halve(block, axis, bit):
    own = (lax.axis_index("dp") & bit) // bit
    keep = lax.dynamic_index_in_dim(block, own, axis, keepdims=True)
    give = lax.dynamic_index_in_dim(block, 1 - own, axis, keepdims=True)
    return add_wide(keep, swap(give, bit))


def sum_tokens(blocks):
    count = len(bits())
    shape = blocks.shape[1:]
    block = blocks.reshape((2,) * count + shape)
    block = halve(block, count - 1, bits()[0])
    parts = jnp.split(block, 2, axis=-1)
    done = []
    for order, part in zip(orders(), parts):
        for bit in order:
            part = halve(part, count - 1 - bits().index(bit), bit)
        done.append(part.reshape(shape[0], -1))
    return jnp.concatenate(done, axis=1)


def reduce_home(part):
    owners, shares = lax.axis_size("dp"), lax.axis_size("expert")
    home = sum_tokens(part.reshape(owners, -1, part.shape[1]))
    me = lax.axis_index("expert")
    width = part.shape[1] // shares
    total = lax.dynamic_slice_in_dim(home, me * width, width, 1).astype(jnp.float32)
    for by in range(1, shares):
        target = lax.rem(me + by, shares)
        sent = lax.dynamic_slice_in_dim(home, target * width, width, 1)
        total = total + shift(sent, by).astype(jnp.float32)
    return total.astype(jnp.bfloat16)


def local(tokens, route_expert, *rest):
    owners = lax.axis_size("dp")
    rows, choose = route_expert.shape
    full = 2 * rows * choose >= owners * rows and owners & (owners - 1) == 0
    return (dense if full else routed)(tokens, route_expert, *rest)


def solution(mesh):
    return jax.shard_map(
        local,
        mesh=mesh,
        in_specs=(
            P("dp", None),
            P("dp", None),
            P("dp", None),
            P("dp", "expert", None),
            P("dp", "expert", None),
            P("dp", "expert", None),
            P("dp", "expert"),
            P("dp", "expert"),
            P(),
            P("dp", "expert"),
        ),
        out_specs=(
            P("dp", "expert"),
            P("dp", "expert"),
            P("dp", None),
            P("dp", "expert", None),
            P("dp", "expert", None),
            P("dp", "expert", None),
        ),
        check_vma=False,
    )
```
